32 devices in a mesh: seq: 4 (over y, x), head: 8 (over z, core).
Axes of the slice: x: 2, y: 2, z: 4, core: 2. Of those that a mesh axis runs over, the one named last changes fastest.
Arguments:
- grad_out: float32 [4096, 1024], P(('seq', 'head')), may hold values from -0.03125 to 0.03125
- features: float32 [4096, 1024], P(('seq', 'head')), may hold values from -6 to 6
- step_size: float32 [4096, 16], P(('seq', 'head')), may hold values from 0.3 to 3
- log_decay: float32 [4096, 16], P(('seq', 'head')), may hold values from -0.85 to 0
- write_proj: float32 [4096, 8, 128], P(('seq', 'head')), may hold values from -6 to 6
- read_proj: float32 [4096, 8, 128], P(('seq', 'head')), may hold values from -6 to 6
Outputs:
- grad_features: float32 [4096, 1024], P(('seq', 'head'))
- grad_write: float32 [4096, 8, 128], P(('seq', 'head'))
- read_gradient: float32 [4096, 8, 128], P(('seq', 'head'))
The draws below stay inside these ranges and needn't reach their ends.
All inputs are finite; a program needn't handle non-finite values.
Results may differ from the reference program's by a relative error of at most 0.00015.
Values sent between devices are 32-bit elements; how exact they have to be, the bound alone decides.
A program may use at most 64 MiB of HBM per device.

```python
import math
import jax
import jax.numpy as jnp
from jax import lax

HEADS = 16
HEAD_SIZE = 64
STATE = 128
GROUPS = 8
SPAN = 256
TOK_DEV = 128
TOKENS = 4096
N_HEAD = 8


def draw_log_decay(key, part):
    key = jax.random.fold_in(key, 7)
    keys = jax.random.split(key, 7)
    keep_share = 0.5
    slow_heads = jax.random.bernoulli(keys[0], keep_share, (HEADS,))
    gentle_decline_factor = jnp.exp(jax.random.uniform(keys[1], (HEADS,), jnp.float32, math.log(0.15), math.log(0.6))) / TOKENS
    fast_rate = jnp.exp(jax.random.uniform(keys[2], (HEADS,), jnp.float32, math.log(1.0 / 50.0), math.log(1.0 / 30.0)))
    head_rate = jnp.where(slow_heads, gentle_decline_factor, fast_rate)
    blocks = TOKENS // TOK_DEV
    block_factor = 2.0 ** jax.random.uniform(keys[3], (blocks, HEADS), jnp.float32, -1.0, 1.0)
    roughness = jnp.exp(jax.random.uniform(keys[4], (TOKENS, HEADS), jnp.float32, -0.5, 0.5))
    regular_fraction = -head_rate[None, :] * jnp.repeat(block_factor, TOK_DEV, axis=0) * roughness
    probe_locations = jax.random.randint(keys[5], (2,), 0, TOKENS)
    stack_levels = jax.random.uniform(keys[6], (2, HEADS), jnp.float32, math.log(1.0 / 0.8), math.log(2.0))
    element_offset_along = jnp.arange(TOKENS)
    spike_clusters = jnp.where(element_offset_along[:, None] == probe_locations[0], stack_levels[0][None, :], 0.0)
    spike_clusters = spike_clusters + jnp.where(element_offset_along[:, None] == probe_locations[1], stack_levels[1][None, :], 0.0)
    return (regular_fraction - spike_clusters).astype(jnp.float32)


def block_scale(key, shape, cuts, low, largest):
    def one(axis_at, shards_of):
        heights = jax.random.uniform(jax.random.fold_in(jax.random.fold_in(key, 6), axis_at), (shards_of,), jnp.float32, low / len(cuts), largest / len(cuts))
        return jnp.repeat(jnp.exp(heights), shape[axis_at] // shards_of).reshape((-1,) + (1,) * (len(shape) - axis_at - 1))

    gain = one(*cuts[0])
    for cut in cuts[1:]:
        gain = gain * one(*cut)
    return gain


def gaussian(stream_key, shape, deviation, limit, shards=(), held_as=jnp.bfloat16):
    entries = deviation * jax.random.normal(stream_key, shape, jnp.float32)
    if shards:
        entries = entries * block_scale(stream_key, shape, shards, -0.22, 0.18)
    return jnp.clip(entries, -limit, limit).astype(held_as)


def setup_inputs(seed: int = 0) -> dict:
    key_of = jax.random.split(jax.random.key(seed), 7)
    grad_out = gaussian(key_of[0], (TOKENS, HEADS * HEAD_SIZE), (1.5 * (STATE * TOKENS) ** -0.5), 0.03125, ((0, 32),), jnp.float32)
    features = gaussian(key_of[1], (TOKENS, HEADS * HEAD_SIZE), 1.0, 6.0, ((0, 32),), jnp.float32)
    step_size = jnp.clip(jnp.exp(math.log(3.0) - 2.3025851 * jax.random.uniform(key_of[2], (TOKENS, HEADS), jnp.float32) ** block_scale(key_of[2], (TOKENS, HEADS), ((0, 32),), -0.2, 0.2)), 0.3, 3.0)
    log_decay = draw_log_decay(jax.random.fold_in(key_of[6], 71), 0)
    write_proj = gaussian(key_of[4], (TOKENS, GROUPS, STATE), 1.0, 6.0, ((0, 32),), jnp.float32)
    read_proj = gaussian(key_of[5], (TOKENS, GROUPS, STATE), 1.0, 6.0, ((0, 32),), jnp.float32)
    return dict(grad_out=grad_out, features=features, step_size=step_size, log_decay=log_decay, write_proj=write_proj, read_proj=read_proj)


PRECISE = lax.Precision.HIGHEST


def summarize(bundle):
    feat_here, grad_here, step_here, decay_here, write_here, read_here = bundle
    per_group = HEADS // GROUPS
    write_heads = jnp.repeat(write_here, per_group, axis=1)
    read_heads = jnp.repeat(read_here, per_group, axis=1)
    cum_log = jnp.cumsum(decay_here, axis=0)
    end_log = cum_log[-1]
    weight_in = step_here * jnp.exp(end_log[None, :] - cum_log)
    fwd_state = jnp.einsum("qhn,qhp->hnp", write_heads * weight_in[:, :, None], feat_here, precision=PRECISE)
    adj_state = jnp.einsum("qhn,qhp->hnp", read_heads * jnp.exp(cum_log)[:, :, None], grad_here, precision=PRECISE)
    return jnp.exp(end_log), fwd_state, adj_state


def block_grads(bundle):
    feat_here, grad_here, step_here, decay_here, write_here, read_here, enter_here, leave_here = bundle
    per_group = HEADS // GROUPS
    write_heads = jnp.repeat(write_here, per_group, axis=1)
    read_heads = jnp.repeat(read_here, per_group, axis=1)
    length = feat_here.shape[0]
    cum_log = jnp.cumsum(decay_here, axis=0)
    end_log = cum_log[-1]
    element_offset_along = jnp.arange(length)
    causal = element_offset_along[:, None] >= element_offset_along[None, :]
    differ = cum_log[:, None, :] - cum_log[None, :, :]
    decay_mat = jnp.exp(jnp.where(causal[:, :, None], differ, -jnp.inf))
    products = jnp.einsum("thp,shp->tsh", grad_here, feat_here, precision=PRECISE) * decay_mat
    matches = jnp.einsum("thn,shn->tsh", read_heads, write_heads, precision=PRECISE) * decay_mat
    to_end = jnp.exp(end_log[None, :] - cum_log)
    from_start = jnp.exp(cum_log)
    read_grad = jnp.einsum("tsh,shn->thn", products * step_here[None, :, :], write_heads, precision=PRECISE)
    read_grad = read_grad + from_start[:, :, None] * jnp.einsum("thp,hnp->thn", grad_here, enter_here, precision=PRECISE)
    write_grad = jnp.einsum("tsh,thn->shn", products, read_heads, precision=PRECISE)
    write_grad = write_grad + to_end[:, :, None] * jnp.einsum("shp,hnp->shn", feat_here, leave_here, precision=PRECISE)
    write_grad = write_grad * step_here[:, :, None]
    feat_grad = jnp.einsum("tsh,thp->shp", matches, grad_here, precision=PRECISE)
    feat_grad = feat_grad + to_end[:, :, None] * jnp.einsum("shn,hnp->shp", write_heads, leave_here, precision=PRECISE)
    feat_grad = feat_grad * step_here[:, :, None]
    write_grad = write_grad.reshape(length, GROUPS, per_group, STATE).sum(axis=2)
    read_grad = read_grad.reshape(length, GROUPS, per_group, STATE).sum(axis=2)
    return feat_grad, write_grad, read_grad


def advance(running, element):
    decay_now, local_now = element
    return decay_now[:, None, None] * running + local_now, running


def reference(grad_out, features, step_size, log_decay, write_proj, read_proj):
    span_len = min(SPAN, TOK_DEV * N_HEAD)
    num_spans = TOKENS // span_len
    feat_blocks = features.reshape(num_spans, span_len, HEADS, HEAD_SIZE)
    grad_blocks = grad_out.reshape(num_spans, span_len, HEADS, HEAD_SIZE)
    step_blocks = step_size.reshape(num_spans, span_len, HEADS)
    decay_blocks = log_decay.reshape(num_spans, span_len, HEADS)
    write_blocks = write_proj.reshape(num_spans, span_len, GROUPS, STATE)
    read_blocks = read_proj.reshape(num_spans, span_len, GROUPS, STATE)
    totals, fwd_states, adj_states = lax.map(summarize, (feat_blocks, grad_blocks, step_blocks, decay_blocks, write_blocks, read_blocks))
    zeros_state = jnp.zeros((HEADS, STATE, HEAD_SIZE), jnp.float32)
    _, enters = lax.scan(advance, zeros_state, (totals, fwd_states))
    _, leaves = lax.scan(advance, zeros_state, (totals, adj_states), reverse=True)
    feat_grad, write_grad, read_grad = lax.map(block_grads, (feat_blocks, grad_blocks, step_blocks, decay_blocks, write_blocks, read_blocks, enters, leaves))
    grad_features = feat_grad.reshape(TOKENS, HEADS * HEAD_SIZE)
    grad_write = write_grad.reshape(TOKENS, GROUPS, STATE)
    read_gradient = read_grad.reshape(TOKENS, GROUPS, STATE)
    return grad_features, grad_write, read_gradient
```

```python
import jax
import jax.numpy as jnp
from jax import lax
from jax.sharding import PartitionSpec as P

PRECISE = lax.Precision.HIGH


def dot(spec, a, b):
    return jnp.einsum(spec, a, b, precision=PRECISE)


def shards(grad_out, features, step_size, log_decay, write_proj, read_proj):
    owners = lax.axis_size("head")
    segs = lax.axis_size("seq")
    q, heads = step_size.shape
    p = grad_out.shape[1] // heads
    groups, n = write_proj.shape[1:]
    per = heads // groups
    mine = heads // owners
    here = lax.axis_index("head")
    seg = lax.axis_index("seq")

    cum = jnp.cumsum(log_decay, axis=0)
    end = cum[-1]
    ends = lax.all_gather(end, ("seq", "head"))
    dy = grad_out.reshape(q, groups, per, p)
    x = features.reshape(q, groups, per, p)
    cum_g = cum.reshape(q, groups, per)
    dt_g = step_size.reshape(q, groups, per)
    from_start = jnp.exp(cum_g)
    to_end = jnp.exp(cum_g[-1:] - cum_g)
    x_in = x * (dt_g * to_end)[..., None]
    dy_in = dy * from_start[..., None]
    fwd = dot("qgn,qghp->ghnp", write_proj, x_in)
    adj = dot("qgn,qghp->ghnp", read_proj, dy_in)
    both = jnp.stack([fwd, adj]).reshape(2, owners, mine, n, p)
    got = lax.all_to_all(both, "head", split_axis=1, concat_axis=1, tiled=True)

    t = jnp.arange(q)
    causal = t[:, None] >= t[None, :]
    ct = jnp.moveaxis(cum_g, 0, 2)
    mat = jnp.exp(jnp.where(causal, ct[..., :, None] - ct[..., None, :], -jnp.inf))
    weighted = (dot("tghp,sghp->ghts", dy, x) * mat * jnp.moveaxis(dt_g, 0, 2)[:, :, None, :]).sum(1)
    matches = dot("tgn,sgn->gts", read_proj, write_proj)[:, None] * mat
    read_grad = dot("gts,sgn->tgn", weighted, write_proj)
    write_grad = dot("gts,tgn->sgn", weighted, read_proj)
    feat_grad = dot("ghts,tghp->sghp", matches, dy)

    logs = lax.dynamic_slice_in_dim(ends, here * mine, mine, 1).reshape(segs, owners, mine)
    seg_log = logs.sum(1)
    dec = jnp.exp(lax.dynamic_index_in_dim(logs, seg, 0, False))[:, :, None, None]
    zero = jnp.zeros((mine, n, p), jnp.float32)
    tf, ta = zero, zero
    for i in range(owners):
        tf = dec[i] * tf + got[0, i]
        k = owners - 1 - i
        ta = dec[k] * ta + got[1, k]
    totals = lax.all_gather(jnp.stack([tf, ta]), "seq")
    sd = jnp.exp(seg_log)[:, :, None, None]
    inc, out = zero, zero
    for s in range(segs - 1):
        inc = jnp.where(s < seg, sd[s] * inc + totals[s, 0], inc)
        k = segs - 1 - s
        out = jnp.where(k > seg, sd[k] * out + totals[k, 1], out)
    enters, leaves = [], []
    for i in range(owners):
        enters.append(inc)
        inc = dec[i] * inc + got[0, i]
        k = owners - 1 - i
        leaves.append(out)
        out = dec[k] * out + got[1, k]
    back = jnp.stack([jnp.stack(enters), jnp.stack(leaves[::-1])])
    back = lax.all_to_all(back, "head", split_axis=1, concat_axis=1, tiled=True)
    back = back.reshape(2, groups, per, n, p)

    read_grad = read_grad + dot("tghp,ghnp->tgn", dy_in, back[0])
    write_grad = write_grad + dot("sghp,ghnp->sgn", x_in, back[1])
    feat_grad = feat_grad + to_end[..., None] * dot("sgn,ghnp->sghp", write_proj, back[1])
    feat_grad = feat_grad * dt_g[..., None]
    return feat_grad.reshape(q, heads * p), write_grad, read_grad


def solution(mesh):
    wide = P(("seq", "head"), None)
    deep = P(("seq", "head"), None, None)
    return jax.shard_map(
        shards,
        mesh=mesh,
        in_specs=(wide, wide, wide, wide, deep, deep),
        out_specs=(wide, deep, deep),
        check_vma=False,
    )
```

```python
import functools

import jax
import jax.numpy as jnp
from jax import lax
from jax.experimental import pallas as pl
from jax.experimental.pallas import tpu as pltpu
from jax.sharding import PartitionSpec as P

MESH = pl.DeviceIdType.MESH
CORES = 2
EXTRA = 8


def split(a):
    high = a.astype(jnp.bfloat16)
    return high, (a - high.astype(jnp.float32)).astype(jnp.bfloat16)


def dot3(a, b, left, right):
    dims = (((left,), (right,)), ((), ()))

    def one(u, v):
        return lax.dot_general(u, v, dims, preferred_element_type=jnp.float32)

    return one(a[0], b[0]) + (one(a[0], b[1]) + one(a[1], b[0]))


def kernel(
    segs, nz, dy_ref, x_ref, dt_ref, la_ref, b_ref, c_ref, feat_ref, write_ref, read_ref,
    send, keep, other, chip, got, total, peers, running, enter, back, back2, xin_ref, dyin_ref,
    ps, pr, zs, zr, ss, sr, bs, br, qs, qr,
):
    q, heads = dt_ref.shape
    groups, n = b_ref.shape[1:]
    per = heads // groups
    p = dy_ref.shape[1] // heads
    lanes = per * p
    gpo = groups // nz
    seg = lax.axis_index("seq")
    head = lax.axis_index("head")
    z, core = head // CORES, lax.rem(head, CORES)
    forward = core == 1
    partner = (seg, z * CORES + (1 - core))

    def along_z(k):
        return lax.rem(z + k + nz, nz)

    def along_seq(k):
        return lax.rem(seg + k + segs, segs)

    def at_z(other_z):
        return (seg, other_z * CORES + core)

    barrier = pltpu.get_barrier_semaphore()
    pl.semaphore_signal(barrier, inc=1, device_id=partner, device_id_type=MESH)
    for k in range(1, nz):
        pl.semaphore_signal(barrier, inc=1, device_id=at_z(along_z(k)), device_id_type=MESH)
    for k in range(1, segs):
        pl.semaphore_signal(barrier, inc=1, device_id=(along_seq(k), head), device_id_type=MESH)

    def copy(src, dst, s_sem, r_sem, device):
        return pltpu.make_async_remote_copy(
            src_ref=src, dst_ref=dst, send_sem=s_sem, recv_sem=r_sem,
            device_id=device, device_id_type=MESH,
        )

    rows = lax.broadcasted_iota(jnp.int32, (q, q), 0)
    cols = lax.broadcasted_iota(jnp.int32, (q, q), 1)
    causal = rows >= cols
    tri = causal.astype(jnp.float32)
    cum = jnp.dot(tri, la_ref[...], precision=lax.Precision.HIGHEST,
                  preferred_element_type=jnp.float32)
    dt = dt_ref[...]
    turned = jnp.concatenate(
        [cum, dt, jnp.zeros((q, q - 2 * heads), jnp.float32)], axis=1).T

    def spread(a, g):
        return jnp.concatenate(
            [jnp.broadcast_to(a[:, h:h + 1], (a.shape[0], p))
             for h in range(g * per, (g + 1) * per)], axis=1)

    def cut(g):
        return slice(g * lanes, (g + 1) * lanes)

    for g in range(groups):
        cum_l = spread(cum, g)
        end_l = cum_l[q - 1:q, :]
        x_in = x_ref[:, cut(g)] * (spread(dt, g) * jnp.exp(end_l - cum_l))
        dy_in = dy_ref[:, cut(g)] * jnp.exp(cum_l)
        xin_ref[:, cut(g)] = x_in
        dyin_ref[:, cut(g)] = dy_in
        fwd = dot3(split(b_ref[:, g, :]), split(x_in), 0, 0)
        adj = dot3(split(c_ref[:, g, :]), split(dy_in), 0, 0)
        log = jnp.broadcast_to(end_l, (EXTRA, lanes))
        send[g, :n, :] = jnp.where(forward, adj, fwd)
        send[g, n:, :] = log
        keep[g, :n, :] = jnp.where(forward, fwd, adj)
        keep[g, n:, :] = log
        if g == 0:
            pl.semaphore_wait(barrier, nz + segs - 1)
        copy(send.at[g], other.at[g], ps.at[g], pr.at[g], partner).start()

    def decayed(log, state, add):
        return jnp.exp(log[0:1, :]) * state + add

    for k in list(range(1, nz)) + [0]:
        owner = along_z(k)
        for j in range(gpo):
            g = owner * gpo + j
            copy(send.at[g], other.at[g], ps.at[g], pr.at[g], partner).wait_recv()
            state = decayed(keep[g, n:, :], other[g, :n, :], keep[g, :n, :])
            log = keep[g, n:, :] + other[g, n:, :]
            if k == 0:
                got[z, j, :n, :] = state
                got[z, j, n:, :] = log
            else:
                chip[g, :n, :] = state
                chip[g, n:, :] = log
                copy(chip.at[g], got.at[z, j], zs.at[k, j], zr.at[z, j], at_z(owner)).start()

    for g in range(groups):
        bs_g, cs_g = split(b_ref[:, g, :]), split(c_ref[:, g, :])
        pairs = dot3(cs_g, bs_g, 1, 1)
        weighted = jnp.zeros((q, q), jnp.float32)
        parts = []
        for h in range(g * per, (g + 1) * per):
            mat = jnp.exp(jnp.where(causal, cum[:, h:h + 1] - turned[h:h + 1, :], -jnp.inf))
            dy_h = split(dy_ref[:, h * p:(h + 1) * p])
            x_h = split(x_ref[:, h * p:(h + 1) * p])
            weighted += dot3(dy_h, x_h, 1, 1) * (mat * turned[heads + h:heads + h + 1, :])
            parts.append(dot3(split(pairs * mat), dy_h, 0, 0))
        w = split(weighted)
        read_ref[:, g, :] = dot3(w, bs_g, 1, 0)
        write_ref[:, g, :] = dot3(w, cs_g, 0, 0)
        feat_ref[:, cut(g)] = jnp.concatenate(parts, axis=1)

    for k in range(1, nz):
        src = along_z(-k)
        for j in range(gpo):
            copy(chip.at[j], got.at[src, j], zs.at[k, j], zr.at[src, j], at_z(src)).wait_recv()

    def place(i):
        return jnp.where(forward, i, nz - 1 - i)

    for j in range(gpo):
        state = got[place(0), j, :n, :]
        log = got[place(0), j, n:, :]
        for i in range(1, nz):
            state = decayed(got[place(i), j, n:, :], state, got[place(i), j, :n, :])
            log = log + got[place(i), j, n:, :]
        total[j, :n, :] = state
        total[j, n:, :] = log

    def feeds(src, dst):
        return jnp.where(forward, dst - src, src - dst) > 0

    for k in range(1, segs):
        dst = along_seq(k)

        @pl.when(feeds(seg, dst))
        def _(k=k, dst=dst):
            copy(total, peers.at[seg], ss.at[k], sr.at[seg], (dst, head)).start()

    running[...] = jnp.zeros_like(running)
    for i in range(segs - 1):
        src = jnp.where(forward, i, segs - 1 - i)

        @pl.when(feeds(src, seg))
        def _(src=src):
            copy(total, peers.at[src], ss.at[0], sr.at[src], (src, head)).wait_recv()
            for j in range(gpo):
                running[j] = decayed(peers[src, j, n:, :], running[j], peers[src, j, :n, :])

    for j in range(gpo):
        state = running[j]
        for i in range(nz):
            enter[place(i), j] = state
            if i < nz - 1:
                state = decayed(got[place(i), j, n:, :], state, got[place(i), j, :n, :])
    for k in range(1, nz):
        dst = along_z(k)
        for j in range(gpo):
            copy(enter.at[dst, j], back.at[z * gpo + j], bs.at[k, j], br.at[z, j],
                 at_z(dst)).start()
    for j in range(gpo):
        back[z * gpo + j] = enter[z, j]
    for k in range(nz):
        src = along_z(-k)
        for j in range(gpo):
            g = src * gpo + j
            if k > 0:
                copy(enter.at[src, j], back.at[g], bs.at[k, j], br.at[src, j],
                     at_z(src)).wait_recv()
            copy(back.at[g], back2.at[g], qs.at[g], qr.at[g], partner).start()

    for g in range(groups):
        copy(back.at[g], back2.at[g], qs.at[g], qr.at[g], partner).wait_recv()
        own = decayed(other[g, n:, :], back[g], other[g, :n, :])
        theirs = back2[g]
        enters = split(jnp.where(forward, own, theirs))
        leaves = split(jnp.where(forward, theirs, own))
        cum_l = spread(cum, g)
        to_end = jnp.exp(cum_l[q - 1:q, :] - cum_l)
        read_ref[:, g, :] += dot3(split(dyin_ref[:, cut(g)]), enters, 1, 1)
        write_ref[:, g, :] += dot3(split(xin_ref[:, cut(g)]), leaves, 1, 1)
        feat_ref[:, cut(g)] = spread(dt, g) * (
            feat_ref[:, cut(g)] + to_end * dot3(split(b_ref[:, g, :]), leaves, 1, 0))

    for g in range(groups):
        copy(send.at[g], other.at[g], ps.at[g], pr.at[g], partner).wait_send()
        copy(back.at[g], back2.at[g], qs.at[g], qr.at[g], partner).wait_send()
    for k in range(1, nz):
        dst = along_z(k)
        for j in range(gpo):
            copy(chip.at[dst * gpo + j], got.at[z, j], zs.at[k, j], zr.at[z, j],
                 at_z(dst)).wait_send()
            copy(enter.at[dst, j], back.at[z * gpo + j], bs.at[k, j], br.at[z, j],
                 at_z(dst)).wait_send()
    for k in range(1, segs):
        dst = along_seq(k)

        @pl.when(feeds(seg, dst))
        def _(k=k, dst=dst):
            copy(total, peers.at[seg], ss.at[k], sr.at[seg], (dst, head)).wait_send()


def shards(segs, owners, *args):
    grad_out, _, step_size, _, write_proj, _ = args
    q, heads = step_size.shape
    groups, n = write_proj.shape[1:]
    lanes = grad_out.shape[1] // groups
    nz = owners // CORES
    gpo = groups // nz
    f32 = jnp.float32
    tall = n + EXTRA
    dma = pltpu.SemaphoreType.DMA
    vmem = pl.BlockSpec(memory_space=pltpu.VMEM)
    return pl.pallas_call(
        functools.partial(kernel, segs, nz),
        out_shape=(
            jax.ShapeDtypeStruct(grad_out.shape, f32),
            jax.ShapeDtypeStruct(write_proj.shape, f32),
            jax.ShapeDtypeStruct(write_proj.shape, f32),
        ),
        in_specs=[vmem] * 6,
        out_specs=(vmem,) * 3,
        scratch_shapes=[
            pltpu.VMEM((groups, tall, lanes), f32),
            pltpu.VMEM((groups, tall, lanes), f32),
            pltpu.VMEM((groups, tall, lanes), f32),
            pltpu.VMEM((groups, tall, lanes), f32),
            pltpu.VMEM((nz, gpo, tall, lanes), f32),
            pltpu.VMEM((gpo, tall, lanes), f32),
            pltpu.VMEM((segs, gpo, tall, lanes), f32),
            pltpu.VMEM((gpo, n, lanes), f32),
            pltpu.VMEM((nz, gpo, n, lanes), f32),
            pltpu.VMEM((groups, n, lanes), f32),
            pltpu.VMEM((groups, n, lanes), f32),
            pltpu.VMEM(grad_out.shape, f32),
            pltpu.VMEM(grad_out.shape, f32),
            dma((groups,)), dma((groups,)),
            dma((nz, gpo)), dma((nz, gpo)),
            dma((segs,)), dma((segs,)),
            dma((nz, gpo)), dma((nz, gpo)),
            dma((groups,)), dma((groups,)),
        ],
        compiler_params=pltpu.CompilerParams(
            collective_id=0, has_side_effects=True, vmem_limit_bytes=48 * 1024 * 1024,
        ),
    )(*args)


def solution(mesh):
    wide = P(("seq", "head"), None)
    deep = P(("seq", "head"), None, None)
    return jax.shard_map(
        functools.partial(shards, mesh.shape["seq"], mesh.shape["head"]),
        mesh=mesh,
        in_specs=(wide, wide, wide, wide, deep, deep),
        out_specs=(wide, deep, deep),
        check_vma=False,
    )
```

```python
import functools

import jax
import jax.numpy as jnp
from jax import lax
from jax.experimental import pallas as pl
from jax.experimental.pallas import tpu as pltpu
from jax.sharding import PartitionSpec as P

MESH = pl.DeviceIdType.MESH
CORES = 2
EXTRA = 8


def split(a):
    high = a.astype(jnp.bfloat16)
    return high, (a - high.astype(jnp.float32)).astype(jnp.bfloat16)


def dot3(a, b, left, right):
    dims = (((left,), (right,)), ((), ()))

    def one(u, v):
        return lax.dot_general(u, v, dims, preferred_element_type=jnp.float32)

    return one(a[0], b[0]) + (one(a[0], b[1]) + one(a[1], b[0]))


def kernel(
    segs, nz, dy_hbm, x_hbm, dt_ref, la_ref, b_hbm, c_hbm, feat_ref, write_ref, read_ref,
    dy_ref, x_ref, b_ref, c_ref, loads,
    send, keep, other, chip, got, total, peers, running, enter, back, back2, xin_ref, dyin_ref,
    ps, pr, zs, zr, ss, sr, bs, br, qs, qr,
):
    fetches = [
        pltpu.make_async_copy(src, dst, loads.at[i])
        for i, (src, dst) in enumerate(
            [(x_hbm, x_ref), (b_hbm, b_ref), (dy_hbm, dy_ref), (c_hbm, c_ref)])
    ]
    for fetch in fetches:
        fetch.start()
    heads, q = dt_ref.shape
    groups, n = b_ref.shape[1:]
    per = heads // groups
    p = dy_ref.shape[1] // heads
    lanes = per * p
    gpo = groups // nz
    seg = lax.axis_index("seq")
    head = lax.axis_index("head")
    z, core = head // CORES, lax.rem(head, CORES)
    forward = core == 1
    partner = (seg, z * CORES + (1 - core))

    def along_z(k):
        return lax.rem(z + k + nz, nz)

    def along_seq(k):
        return lax.rem(seg + k + segs, segs)

    def at_z(other_z):
        return (seg, other_z * CORES + core)

    barrier = pltpu.get_barrier_semaphore()
    pl.semaphore_signal(barrier, inc=1, device_id=partner, device_id_type=MESH)
    for k in range(1, nz):
        pl.semaphore_signal(barrier, inc=1, device_id=at_z(along_z(k)), device_id_type=MESH)
    for k in range(1, segs):
        pl.semaphore_signal(barrier, inc=1, device_id=(along_seq(k), head), device_id_type=MESH)

    def copy(src, dst, s_sem, r_sem, device):
        return pltpu.make_async_remote_copy(
            src_ref=src, dst_ref=dst, send_sem=s_sem, recv_sem=r_sem,
            device_id=device, device_id_type=MESH,
        )

    rows = lax.broadcasted_iota(jnp.int32, (q, q), 0)
    cols = lax.broadcasted_iota(jnp.int32, (q, q), 1)
    causal = rows >= cols
    upto = (rows <= cols).astype(jnp.float32)
    cum_t = jnp.dot(la_ref[...], upto, precision=lax.Precision.HIGHEST,
                    preferred_element_type=jnp.float32)
    turned = jnp.concatenate(
        [cum_t, dt_ref[...], jnp.zeros((q - 2 * heads, q), jnp.float32)], axis=0)
    upright = turned.T
    cum, dt = upright[:, :heads], upright[:, heads:2 * heads]

    def spread(a, g):
        return jnp.concatenate(
            [jnp.broadcast_to(a[:, h:h + 1], (a.shape[0], p))
             for h in range(g * per, (g + 1) * per)], axis=1)

    def cut(g):
        return slice(g * lanes, (g + 1) * lanes)

    def decayed(log, state, add):
        return jnp.exp(log[0:1, :]) * state + add

    def chunk_states(g):
        cum_l = spread(cum, g)
        end_l = cum_l[q - 1:q, :]
        x_in = x_ref[:, cut(g)] * (spread(dt, g) * jnp.exp(end_l - cum_l))
        dy_in = dy_ref[:, cut(g)] * jnp.exp(cum_l)
        xin_ref[:, cut(g)] = x_in
        dyin_ref[:, cut(g)] = dy_in
        fwd = dot3(split(b_ref[:, g, :]), split(x_in), 0, 0)
        adj = dot3(split(c_ref[:, g, :]), split(dy_in), 0, 0)
        log = jnp.broadcast_to(end_l, (EXTRA, lanes))
        send[g, :n, :] = jnp.where(forward, adj, fwd)
        send[g, n:, :] = log
        keep[g, :n, :] = jnp.where(forward, fwd, adj)
        keep[g, n:, :] = log

    def chip_state(g):
        owner, j = g // gpo, g % gpo
        copy(send.at[g], other.at[g], ps.at[g], pr.at[g], partner).wait_recv()
        state = decayed(keep[g, n:, :], other[g, :n, :], keep[g, :n, :])
        log = keep[g, n:, :] + other[g, n:, :]

        @pl.when(z == owner)
        def _():
            got[z, j, :n, :] = state
            got[z, j, n:, :] = log

        @pl.when(z != owner)
        def _():
            chip[g, :n, :] = state
            chip[g, n:, :] = log
            copy(chip.at[g], got.at[z, j], zs.at[g], zr.at[z, j], at_z(owner)).start()

    mixed = [o for pair in zip(range(nz // 2), range(nz // 2, nz)) for o in pair]
    order = [o * gpo + j for j in range(gpo) for o in mixed]
    lag = 2
    for fetch in fetches:
        fetch.wait()
    for i, g in enumerate(order):
        chunk_states(g)
        if i == 0:
            pl.semaphore_wait(barrier, nz + segs - 1)
        copy(send.at[g], other.at[g], ps.at[g], pr.at[g], partner).start()
        if i >= lag:
            chip_state(order[i - lag])
    for g in order[len(order) - lag:]:
        chip_state(g)

    def within(g):
        bs_g, cs_g = split(b_ref[:, g, :]), split(c_ref[:, g, :])
        pairs = dot3(cs_g, bs_g, 1, 1)
        weighted = jnp.zeros((q, q), jnp.float32)
        parts = []
        for h in range(g * per, (g + 1) * per):
            mat = jnp.exp(jnp.where(causal, cum[:, h:h + 1] - turned[h:h + 1, :], -jnp.inf))
            dy_h = split(dy_ref[:, h * p:(h + 1) * p])
            x_h = split(x_ref[:, h * p:(h + 1) * p])
            weighted += dot3(dy_h, x_h, 1, 1) * (mat * turned[heads + h:heads + h + 1, :])
            parts.append(dot3(split(pairs * mat), dy_h, 0, 0))
        w = split(weighted)
        read_ref[:, g, :] = dot3(w, bs_g, 1, 0)
        write_ref[:, g, :] = dot3(w, cs_g, 0, 0)
        feat_ref[:, cut(g)] = jnp.concatenate(parts, axis=1)

    def place(i):
        return jnp.where(forward, i, nz - 1 - i)

    def feeds(src, dst):
        return jnp.where(forward, dst - src, src - dst) > 0

    half, most = groups // 2, groups * 3 // 4
    for g in range(half):
        within(g)

    for j in range(gpo):
        for k in range(1, nz):
            src = along_z(-k)
            copy(chip.at[j], got.at[src, j], zs.at[j], zr.at[src, j], at_z(src)).wait_recv()
        state = got[place(0), j, :n, :]
        log = got[place(0), j, n:, :]
        for i in range(1, nz):
            state = decayed(got[place(i), j, n:, :], state, got[place(i), j, :n, :])
            log = log + got[place(i), j, n:, :]
        total[j, :n, :] = state
        total[j, n:, :] = log
        for k in range(1, segs):
            dst = along_seq(k)

            @pl.when(feeds(seg, dst))
            def _(k=k, dst=dst, j=j):
                copy(total.at[j], peers.at[seg, j], ss.at[k, j], sr.at[seg, j],
                     (dst, head)).start()

    for g in range(half, most):
        within(g)

    running[...] = jnp.zeros_like(running)
    for j in range(gpo):
        for i in range(segs - 1):
            src = jnp.where(forward, i, segs - 1 - i)

            @pl.when(feeds(src, seg))
            def _(src=src, j=j):
                copy(total.at[j], peers.at[src, j], ss.at[0, j], sr.at[src, j],
                     (src, head)).wait_recv()
                running[j] = decayed(peers[src, j, n:, :], running[j], peers[src, j, :n, :])

        state = running[j]
        for i in range(nz):
            enter[place(i), j] = state
            if i < nz - 1:
                state = decayed(got[place(i), j, n:, :], state, got[place(i), j, :n, :])
        for k in range(1, nz):
            dst = along_z(k)
            copy(enter.at[dst, j], back.at[z * gpo + j], bs.at[k, j], br.at[z, j],
                 at_z(dst)).start()
        mine = z * gpo + j
        back[mine] = enter[z, j]
        copy(back.at[mine], back2.at[mine], qs.at[mine], qr.at[mine], partner).start()

    for g in range(most, groups):
        within(g)

    def hand_on(g):
        owner, j = g // gpo, g % gpo

        @pl.when(z != owner)
        def _():
            copy(enter.at[owner, j], back.at[g], bs.at[1, j], br.at[owner, j],
                 at_z(owner)).wait_recv()
            copy(back.at[g], back2.at[g], qs.at[g], qr.at[g], partner).start()

    def finish(g):
        copy(back.at[g], back2.at[g], qs.at[g], qr.at[g], partner).wait_recv()
        own = decayed(other[g, n:, :], back[g], other[g, :n, :])
        theirs = back2[g]
        enters = split(jnp.where(forward, own, theirs))
        leaves = split(jnp.where(forward, theirs, own))
        cum_l = spread(cum, g)
        to_end = jnp.exp(cum_l[q - 1:q, :] - cum_l)
        read_ref[:, g, :] += dot3(split(dyin_ref[:, cut(g)]), enters, 1, 1)
        write_ref[:, g, :] += dot3(split(xin_ref[:, cut(g)]), leaves, 1, 1)
        feat_ref[:, cut(g)] = spread(dt, g) * (
            feat_ref[:, cut(g)] + to_end * dot3(split(b_ref[:, g, :]), leaves, 1, 0))

    for i, g in enumerate(order):
        hand_on(g)
        if i >= lag:
            finish(order[i - lag])
    for g in order[len(order) - lag:]:
        finish(g)

    for g in range(groups):
        copy(send.at[g], other.at[g], ps.at[g], pr.at[g], partner).wait_send()
        copy(back.at[g], back2.at[g], qs.at[g], qr.at[g], partner).wait_send()
        owner, j = g // gpo, g % gpo

        @pl.when(z != owner)
        def _(g=g, owner=owner, j=j):
            copy(chip.at[g], got.at[z, j], zs.at[g], zr.at[z, j], at_z(owner)).wait_send()

    for j in range(gpo):
        for k in range(1, nz):
            dst = along_z(k)
            copy(enter.at[dst, j], back.at[z * gpo + j], bs.at[k, j], br.at[z, j],
                 at_z(dst)).wait_send()
        for k in range(1, segs):
            dst = along_seq(k)

            @pl.when(feeds(seg, dst))
            def _(k=k, dst=dst, j=j):
                copy(total.at[j], peers.at[seg, j], ss.at[k, j], sr.at[seg, j],
                     (dst, head)).wait_send()


def shards(segs, owners, *args):
    grad_out, features, step_size, log_decay, write_proj, read_proj = args
    groups, n = write_proj.shape[1:]
    lanes = grad_out.shape[1] // groups
    nz = owners // CORES
    gpo = groups // nz
    f32 = jnp.float32
    tall = n + EXTRA
    dma = pltpu.SemaphoreType.DMA
    vmem = pl.BlockSpec(memory_space=pltpu.VMEM)
    whole = pl.BlockSpec(memory_space=pl.ANY)
    return pl.pallas_call(
        functools.partial(kernel, segs, nz),
        out_shape=(
            jax.ShapeDtypeStruct(grad_out.shape, f32),
            jax.ShapeDtypeStruct(write_proj.shape, f32),
            jax.ShapeDtypeStruct(write_proj.shape, f32),
        ),
        in_specs=[whole, whole, vmem, vmem, whole, whole],
        out_specs=(vmem,) * 3,
        scratch_shapes=[
            pltpu.VMEM(grad_out.shape, f32),
            pltpu.VMEM(grad_out.shape, f32),
            pltpu.VMEM(write_proj.shape, f32),
            pltpu.VMEM(write_proj.shape, f32),
            dma((4,)),
            pltpu.VMEM((groups, tall, lanes), f32),
            pltpu.VMEM((groups, tall, lanes), f32),
            pltpu.VMEM((groups, tall, lanes), f32),
            pltpu.VMEM((groups, tall, lanes), f32),
            pltpu.VMEM((nz, gpo, tall, lanes), f32),
            pltpu.VMEM((gpo, tall, lanes), f32),
            pltpu.VMEM((segs, gpo, tall, lanes), f32),
            pltpu.VMEM((gpo, n, lanes), f32),
            pltpu.VMEM((nz, gpo, n, lanes), f32),
            pltpu.VMEM((groups, n, lanes), f32),
            pltpu.VMEM((groups, n, lanes), f32),
            pltpu.VMEM(grad_out.shape, f32),
            pltpu.VMEM(grad_out.shape, f32),
            dma((groups,)), dma((groups,)),
            dma((groups,)), dma((nz, gpo)),
            dma((segs, gpo)), dma((segs, gpo)),
            dma((nz, gpo)), dma((nz, gpo)),
            dma((groups,)), dma((groups,)),
        ],
        compiler_params=pltpu.CompilerParams(
            collective_id=0, has_side_effects=True, vmem_limit_bytes=56 * 1024 * 1024,
        ),
    )(grad_out, features, step_size.T, log_decay.T, write_proj, read_proj)


def solution(mesh):
    wide = P(("seq", "head"), None)
    deep = P(("seq", "head"), None, None)
    return jax.shard_map(
        functools.partial(shards, mesh.shape["seq"], mesh.shape["head"]),
        mesh=mesh,
        in_specs=(wide, wide, wide, wide, deep, deep),
        out_specs=(wide, deep, deep),
        check_vma=False,
    )
```

```python
import functools

import jax
import jax.numpy as jnp
from jax import lax
from jax.experimental import pallas as pl
from jax.experimental.pallas import tpu as pltpu
from jax.sharding import PartitionSpec as P

MESH = pl.DeviceIdType.MESH
CORES = 2
EXTRA = 8


def split(a):
    high = a.astype(jnp.bfloat16)
    return high, (a - high.astype(jnp.float32)).astype(jnp.bfloat16)


def dot3(a, b, left, right):
    dims = (((left,), (right,)), ((), ()))

    def one(u, v):
        return lax.dot_general(u, v, dims, preferred_element_type=jnp.float32)

    return one(a[0], b[0]) + (one(a[0], b[1]) + one(a[1], b[0]))


def kernel(
    segs, nz, dy_hbm, x_hbm, dt_ref, la_ref, b_hbm, c_hbm, feat_ref, write_ref, read_ref,
    dy_ref, x_ref, b_ref, c_ref, loads,
    send, keep, other, chip, got, total, peers, running, enter, back, back2, xin_ref, dyin_ref,
    ps, pr, zs, zr, ss, sr, bs, br, qs, qr,
):
    fetches = [
        pltpu.make_async_copy(src, dst, loads.at[i])
        for i, (src, dst) in enumerate(
            [(x_hbm, x_ref), (b_hbm, b_ref), (dy_hbm, dy_ref), (c_hbm, c_ref)])
    ]
    for fetch in fetches:
        fetch.start()
    heads, q = dt_ref.shape
    groups, n = b_ref.shape[1:]
    per = heads // groups
    p = dy_ref.shape[1] // heads
    lanes = per * p
    gpo = groups // nz
    seg = lax.axis_index("seq")
    head = lax.axis_index("head")
    z, core = head // CORES, lax.rem(head, CORES)
    forward = core == 1
    partner = (seg, z * CORES + (1 - core))

    def along_z(k):
        return lax.rem(z + k + nz, nz)

    def along_seq(k):
        return lax.rem(seg + k + segs, segs)

    def at_z(other_z):
        return (seg, other_z * CORES + core)

    barrier = pltpu.get_barrier_semaphore()
    pl.semaphore_signal(barrier, inc=1, device_id=partner, device_id_type=MESH)
    for k in range(1, nz):
        pl.semaphore_signal(barrier, inc=1, device_id=at_z(along_z(k)), device_id_type=MESH)
    for k in range(1, segs):
        pl.semaphore_signal(barrier, inc=1, device_id=(along_seq(k), head), device_id_type=MESH)

    def copy(src, dst, s_sem, r_sem, device):
        return pltpu.make_async_remote_copy(
            src_ref=src, dst_ref=dst, send_sem=s_sem, recv_sem=r_sem,
            device_id=device, device_id_type=MESH,
        )

    rows = lax.broadcasted_iota(jnp.int32, (q, q), 0)
    cols = lax.broadcasted_iota(jnp.int32, (q, q), 1)
    causal = rows >= cols
    upto = (rows <= cols).astype(jnp.float32)
    cum_t = jnp.dot(la_ref[...], upto, precision=lax.Precision.HIGHEST,
                    preferred_element_type=jnp.float32)
    turned = jnp.concatenate(
        [cum_t, dt_ref[...], jnp.zeros((q - 2 * heads, q), jnp.float32)], axis=0)
    upright = turned.T
    cum, dt = upright[:, :heads], upright[:, heads:2 * heads]

    def spread(a, g):
        return jnp.concatenate(
            [jnp.broadcast_to(a[:, h:h + 1], (a.shape[0], p))
             for h in range(g * per, (g + 1) * per)], axis=1)

    def cut(g):
        return slice(g * lanes, (g + 1) * lanes)

    def decayed(log, state, add):
        return jnp.exp(log[0:1, :]) * state + add

    def chunk_states(g):
        cum_l = spread(cum, g)
        end_l = cum_l[q - 1:q, :]
        x_in = x_ref[:, cut(g)] * (spread(dt, g) * jnp.exp(end_l - cum_l))
        dy_in = dy_ref[:, cut(g)] * jnp.exp(cum_l)
        xin_ref[:, cut(g)] = x_in
        dyin_ref[:, cut(g)] = dy_in
        fwd = dot3(split(b_ref[:, g, :]), split(x_in), 0, 0)
        adj = dot3(split(c_ref[:, g, :]), split(dy_in), 0, 0)
        log = jnp.broadcast_to(end_l, (EXTRA, lanes))
        send[g, :n, :] = jnp.where(forward, adj, fwd)
        send[g, n:, :] = log
        keep[g, :n, :] = jnp.where(forward, fwd, adj)
        keep[g, n:, :] = log

    def chip_state(g):
        owner, j = g // gpo, g % gpo
        copy(send.at[g], other.at[g], ps.at[g], pr.at[g], partner).wait_recv()
        state = decayed(keep[g, n:, :], other[g, :n, :], keep[g, :n, :])
        log = keep[g, n:, :] + other[g, n:, :]

        @pl.when(z == owner)
        def _():
            got[z, j, :n, :] = state
            got[z, j, n:, :] = log

        @pl.when(z != owner)
        def _():
            chip[g, :n, :] = state
            chip[g, n:, :] = log
            copy(chip.at[g], got.at[z, j], zs.at[g], zr.at[z, j], at_z(owner)).start()

    mixed = [o for pair in zip(range(nz // 2), range(nz // 2, nz)) for o in pair]
    order = [o * gpo + j for j in range(gpo) for o in mixed]
    lag = 2
    for fetch in fetches:
        fetch.wait()
    for i, g in enumerate(order):
        chunk_states(g)
        if i == 0:
            pl.semaphore_wait(barrier, nz + segs - 1)
        copy(send.at[g], other.at[g], ps.at[g], pr.at[g], partner).start()
        if i >= lag:
            chip_state(order[i - lag])
    for g in order[len(order) - lag:]:
        chip_state(g)

    def within(g):
        bs_g, cs_g = split(b_ref[:, g, :]), split(c_ref[:, g, :])
        pairs = dot3(cs_g, bs_g, 1, 1)
        weighted = jnp.zeros((q, q), jnp.float32)
        parts = []
        for h in range(g * per, (g + 1) * per):
            mat = jnp.exp(jnp.where(causal, cum[:, h:h + 1] - turned[h:h + 1, :], -jnp.inf))
            dy_h = split(dy_ref[:, h * p:(h + 1) * p])
            x_h = split(x_ref[:, h * p:(h + 1) * p])
            weighted += dot3(dy_h, x_h, 1, 1) * (mat * turned[heads + h:heads + h + 1, :])
            parts.append(dot3(split(pairs * mat), dy_h, 0, 0))
        w = split(weighted)
        read_ref[:, g, :] = dot3(w, bs_g, 1, 0)
        write_ref[:, g, :] = dot3(w, cs_g, 0, 0)
        feat_ref[:, cut(g)] = jnp.concatenate(parts, axis=1)

    def place(i):
        return jnp.where(forward, i, nz - 1 - i)

    def feeds(src, dst):
        return jnp.where(forward, dst - src, src - dst) > 0

    half, most = groups // 2, groups * 3 // 4
    for g in range(half):
        within(g)

    for j in range(gpo):
        for k in range(1, nz):
            src = along_z(-k)
            copy(chip.at[j], got.at[src, j], zs.at[j], zr.at[src, j], at_z(src)).wait_recv()
        state = got[place(0), j, :n, :]
        log = got[place(0), j, n:, :]
        for i in range(1, nz):
            state = decayed(got[place(i), j, n:, :], state, got[place(i), j, :n, :])
            log = log + got[place(i), j, n:, :]
        total[j, :n, :] = state
        total[j, n:, :] = log
        for k in range(1, segs):
            dst = along_seq(k)

            @pl.when(feeds(seg, dst))
            def _(k=k, dst=dst, j=j):
                copy(total.at[j], peers.at[seg, j], ss.at[k, j], sr.at[seg, j],
                     (dst, head)).start()

    for g in range(half, most):
        within(g)

    running[...] = jnp.zeros_like(running)
    for j in range(gpo):
        for i in range(segs - 1):
            src = jnp.where(forward, i, segs - 1 - i)

            @pl.when(feeds(src, seg))
            def _(src=src, j=j):
                copy(total.at[j], peers.at[src, j], ss.at[0, j], sr.at[src, j],
                     (src, head)).wait_recv()
                running[j] = decayed(peers[src, j, n:, :], running[j], peers[src, j, :n, :])

        state = running[j]
        for i in range(nz):
            enter[place(i), j] = state
            if i < nz - 1:
                state = decayed(got[place(i), j, n:, :], state, got[place(i), j, :n, :])
        for k in range(1, nz):
            dst = along_z(k)
            copy(enter.at[dst, j], back.at[z * gpo + j], bs.at[k, j], br.at[z, j],
                 at_z(dst)).start()
        mine = z * gpo + j
        back[mine] = enter[z, j]
        copy(back.at[mine], back2.at[mine], qs.at[mine], qr.at[mine], partner).start()

    for g in range(most, groups):
        within(g)

    def hand_on(g):
        owner, j = g // gpo, g % gpo

        @pl.when(z != owner)
        def _():
            copy(enter.at[owner, j], back.at[g], bs.at[1, j], br.at[owner, j],
                 at_z(owner)).wait_recv()
            copy(back.at[g], back2.at[g], qs.at[g], qr.at[g], partner).start()

    def finish(g):
        copy(back.at[g], back2.at[g], qs.at[g], qr.at[g], partner).wait_recv()
        own = decayed(other[g, n:, :], back[g], other[g, :n, :])
        theirs = back2[g]
        enters = split(jnp.where(forward, own, theirs))
        leaves = split(jnp.where(forward, theirs, own))
        cum_l = spread(cum, g)
        to_end = jnp.exp(cum_l[q - 1:q, :] - cum_l)
        read_ref[:, g, :] += dot3(split(dyin_ref[:, cut(g)]), enters, 1, 1)
        write_ref[:, g, :] += dot3(split(xin_ref[:, cut(g)]), leaves, 1, 1)
        feat_ref[:, cut(g)] = spread(dt, g) * (
            feat_ref[:, cut(g)] + to_end * dot3(split(b_ref[:, g, :]), leaves, 1, 0))

    for i, g in enumerate(order):
        hand_on(g)
        if i >= lag:
            finish(order[i - lag])
    for g in order[len(order) - lag:]:
        finish(g)

    for g in range(groups):
        copy(send.at[g], other.at[g], ps.at[g], pr.at[g], partner).wait_send()
        copy(back.at[g], back2.at[g], qs.at[g], qr.at[g], partner).wait_send()
        owner, j = g // gpo, g % gpo

        @pl.when(z != owner)
        def _(g=g, owner=owner, j=j):
            copy(chip.at[g], got.at[z, j], zs.at[g], zr.at[z, j], at_z(owner)).wait_send()

    for j in range(gpo):
        for k in range(1, nz):
            dst = along_z(k)
            copy(enter.at[dst, j], back.at[z * gpo + j], bs.at[k, j], br.at[z, j],
                 at_z(dst)).wait_send()
        for k in range(1, segs):
            dst = along_seq(k)

            @pl.when(feeds(seg, dst))
            def _(k=k, dst=dst, j=j):
                copy(total.at[j], peers.at[seg, j], ss.at[k, j], sr.at[seg, j],
                     (dst, head)).wait_send()


def deliver(a_in, b_in, c_in, a_out, b_out, c_out):
    a_out[...] = a_in[...]
    b_out[...] = b_in[...]
    c_out[...] = c_in[...]


def shards(segs, owners, *args):
    grad_out, features, step_size, log_decay, write_proj, read_proj = args
    groups, n = write_proj.shape[1:]
    lanes = grad_out.shape[1] // groups
    nz = owners // CORES
    gpo = groups // nz
    f32 = jnp.float32
    tall = n + EXTRA
    dma = pltpu.SemaphoreType.DMA
    vmem = pl.BlockSpec(memory_space=pltpu.VMEM)
    whole = pl.BlockSpec(memory_space=pl.ANY)
    grads = pl.pallas_call(
        functools.partial(kernel, segs, nz),
        out_shape=(
            jax.ShapeDtypeStruct(grad_out.shape, f32),
            jax.ShapeDtypeStruct(write_proj.shape, f32),
            jax.ShapeDtypeStruct(write_proj.shape, f32),
        ),
        in_specs=[whole, whole, vmem, vmem, whole, whole],
        out_specs=(vmem,) * 3,
        scratch_shapes=[
            pltpu.VMEM(grad_out.shape, f32),
            pltpu.VMEM(grad_out.shape, f32),
            pltpu.VMEM(write_proj.shape, f32),
            pltpu.VMEM(write_proj.shape, f32),
            dma((4,)),
            pltpu.VMEM((groups, tall, lanes), f32),
            pltpu.VMEM((groups, tall, lanes), f32),
            pltpu.VMEM((groups, tall, lanes), f32),
            pltpu.VMEM((groups, tall, lanes), f32),
            pltpu.VMEM((nz, gpo, tall, lanes), f32),
            pltpu.VMEM((gpo, tall, lanes), f32),
            pltpu.VMEM((segs, gpo, tall, lanes), f32),
            pltpu.VMEM((gpo, n, lanes), f32),
            pltpu.VMEM((nz, gpo, n, lanes), f32),
            pltpu.VMEM((groups, n, lanes), f32),
            pltpu.VMEM((groups, n, lanes), f32),
            pltpu.VMEM(grad_out.shape, f32),
            pltpu.VMEM(grad_out.shape, f32),
            dma((groups,)), dma((groups,)),
            dma((groups,)), dma((nz, gpo)),
            dma((segs, gpo)), dma((segs, gpo)),
            dma((nz, gpo)), dma((nz, gpo)),
            dma((groups,)), dma((groups,)),
        ],
        compiler_params=pltpu.CompilerParams(
            collective_id=0, has_side_effects=True, vmem_limit_bytes=56 * 1024 * 1024,
        ),
    )(grad_out, features, step_size.T, log_decay.T, write_proj, read_proj)
    steps = 2
    blocks = [
        pl.BlockSpec((g.shape[0] // steps,) + g.shape[1:], lambda i, r=g.ndim: (i,) + (0,) * (r - 1))
        for g in grads
    ]
    return pl.pallas_call(
        deliver,
        grid=(steps,),
        out_shape=tuple(jax.ShapeDtypeStruct(g.shape, f32) for g in grads),
        in_specs=blocks,
        out_specs=tuple(blocks),
        compiler_params=pltpu.CompilerParams(vmem_limit_bytes=56 * 1024 * 1024),
    )(*grads)


def solution(mesh):
    wide = P(("seq", "head"), None)
    deep = P(("seq", "head"), None, None)
    return jax.shard_map(
        functools.partial(shards, mesh.shape["seq"], mesh.shape["head"]),
        mesh=mesh,
        in_specs=(wide, wide, wide, wide, deep, deep),
        out_specs=(wide, deep, deep),
        check_vma=False,
    )
```
